128 devices in a mesh: section: 2 (over x_hi), row: 8 (over z, x_lo), col: 8 (over y, core).
Axes of the slice: x: 4 (x_hi: 2, x_lo: 2; x = x_hi * 2 + x_lo), y: 4, z: 4, core: 2. Of those that a mesh axis runs over, the one named last changes fastest.
Arguments:
- tokens: bfloat16 [2, 512, 12288], P('section', 'row', 'col'), may hold values from -6 to 6
- cotangent: bfloat16 [2, 512, 12288], P('section', 'row', 'col'), may hold values from -6 to 6
- w_in: bfloat16 [2, 12288, 24576], P('section', 'col', 'row'), may hold values from -0.0546875 to 0.0546875
- b_in: float32 [2, 24576], P('section', 'row'), may hold values from -3 to 3
- w_out: bfloat16 [2, 24576, 12288], P('section', 'row', 'col'), may hold values from -0.0390625 to 0.0390625
- b_out: float32 [2, 12288], P('section', 'col'), may hold values from -3 to 3
Outputs:
- handed_over: float32 [2, 512, 12288], P('section', 'row', 'col')
- leaving: bfloat16 [2, 512, 12288], P('section', 'row', 'col')
The draws below stay inside these ranges and needn't reach their ends.
All inputs are finite; a program needn't handle non-finite values.
Results may differ from the reference program's by a relative error of at most 0.019.
Values may be sent and summed in bfloat16 or wider, within the bound.
A program may use at most 128 MiB of HBM per device.

```python
import math
import jax
import jax.numpy as jnp
from jax import lax

D = 12288
FFW = 24576
HB = 128
TOKENS = 512
SECTIONS = 2
N_ROW = 8
N_COL = 8


def shard_levels(own_key, shape, cuts, smallest, largest):
    gain = 1.0
    for position, shards_of in cuts:
        heights = jax.random.uniform(jax.random.fold_in(jax.random.fold_in(own_key, 6), position), (shards_of,), jnp.float32, smallest / len(cuts), largest / len(cuts))
        gain = gain * jnp.repeat(jnp.exp(heights), shape[position] // shards_of).reshape((-1,) + (1,) * (len(shape) - 1 - position))
    return gain


def centred(rng, extent, width, bound, split=(), kind=jnp.bfloat16):
    level = shard_levels(rng, extent, split, -0.22, 0.18) if split else 1.0
    entries = jax.random.normal(rng, extent, jnp.float32) * width * level
    return jnp.minimum(jnp.maximum(entries, -bound), bound).astype(kind)


def setup_inputs(seed: int = 0) -> dict:
    seeds = jax.random.split(jax.random.key(seed), 7)
    tokens = centred(seeds[0], (SECTIONS, TOKENS, D), 1.0, 6.0, ((0, 2), (1, 8), (2, 8)))
    cotangent = centred(seeds[1], (SECTIONS, TOKENS, D), 1.0, 6.0, ((0, 2), (1, 8), (2, 8)))
    w_in = centred(seeds[2], (SECTIONS, D, FFW), D ** -0.5, 0.0546875, ((0, 2), (1, 8), (2, 8)))
    b_in = centred(seeds[3], (SECTIONS, FFW), 0.5, 3.0, ((0, 2), (1, 8)), jnp.float32)
    w_out = centred(seeds[4], (SECTIONS, FFW, D), FFW ** -0.5, 0.0390625, ((0, 2), (1, 8), (2, 8)))
    b_out = centred(seeds[5], (SECTIONS, D), 0.5, 3.0, ((0, 2), (1, 8)), jnp.float32)
    return dict(tokens=tokens, cotangent=cotangent, w_in=w_in, b_in=b_in, w_out=w_out, b_out=b_out)


def hadamard_table(length):
    index = jnp.arange(length, dtype=jnp.int32)
    signs = jnp.ones((length, length), jnp.float32)
    level = 1
    while level < length:
        bit_set = index // level % 2
        signs = signs * (1.0 - 2.0 * (bit_set[:, None] * bit_set[None, :]).astype(jnp.float32))
        level = level * 2
    return signs / math.sqrt(length)

def rotate(field, rotation):
    blocks = field.reshape(field.shape[:-1] + (field.shape[-1] // HB, HB))
    turned = jnp.einsum('tbk,kj->tbj', blocks, rotation, precision=lax.Precision.HIGHEST)
    return turned.reshape(field.shape)

def gelu_parts(pre_act):
    factor = math.sqrt(2.0 / math.pi)
    tangent = jnp.tanh(factor * (pre_act + 0.044715 * pre_act * pre_act * pre_act))
    values = 0.5 * pre_act * (1.0 + tangent)
    slopes = 0.5 * (1.0 + tangent) + 0.5 * pre_act * (1.0 - tangent * tangent) * factor * (1.0 + 3.0 * 0.044715 * pre_act * pre_act)
    return (values, slopes)

def split_dot(leading, trailing, pieces):
    block_width = leading.shape[1] // pieces
    summed = jnp.zeros((leading.shape[0], trailing.shape[1]), jnp.float32)
    for index in range(pieces):
        partial_value = jnp.dot(leading[:, index * block_width:(index + 1) * block_width], trailing[index * block_width:(index + 1) * block_width], preferred_element_type=jnp.float32)
        rounded = lax.optimization_barrier(partial_value.astype(jnp.bfloat16))
        summed = summed + rounded.astype(jnp.float32)
    return summed

def section_pass(tok_in, grad_out, w_first, b_first, w_second, b_second):
    pre_act = split_dot(tok_in, w_first, N_COL) + b_first
    values, slopes = gelu_parts(pre_act)
    active = values.astype(jnp.bfloat16)
    output = tok_in.astype(jnp.float32) + split_dot(active, w_second, N_ROW) + b_second
    back_sum = split_dot(grad_out, w_second.T, N_COL)
    grad_hidden = (back_sum * slopes).astype(jnp.bfloat16)
    grad_in = grad_out.astype(jnp.float32) + split_dot(grad_hidden, w_first.T, N_ROW)
    return (output, grad_in)

def reference(tokens, cotangent, w_in, b_in, w_out, b_out):
    rotation = hadamard_table(HB)
    out_first, grad_first = section_pass(tokens[0], cotangent[0], w_in[0], b_in[0], w_out[0], b_out[0])
    out_second, grad_second = section_pass(tokens[1], cotangent[1], w_in[1], b_in[1], w_out[1], b_out[1])
    sent_back = lax.optimization_barrier(rotate(grad_second, rotation).astype(jnp.bfloat16))
    sent_forth = lax.optimization_barrier(rotate(out_first, rotation).astype(jnp.bfloat16))
    handed_over = jnp.stack([rotate(sent_back.astype(jnp.float32), rotation), rotate(sent_forth.astype(jnp.float32), rotation)])
    leaving = jnp.stack([grad_first.astype(jnp.bfloat16), out_second.astype(jnp.bfloat16)])
    return (handed_over, leaving)
```

```python
import functools
import math

import jax
import jax.numpy as jnp
import numpy as np
from jax import lax
from jax.experimental import pallas as pl
from jax.experimental.pallas import tpu as pltpu
from jax.sharding import PartitionSpec as P

HB = 128
W = 1536
TN = 768
BF = jnp.bfloat16
F32 = jnp.float32


PAIRS = ((0, 32, 2, (1, 1)), (32, 32, 2, (2, 2)))
FORWARD, BACKWARD = 0, 1
GOES, STAYS = 0, 1
SEMAPHORES = 320

PHASES = (
    "ag1", "ag1b", "ag2a", "ag2b", "ag3", "ag4", "a1", "a2", "rs1", "rs2", "rs3", "yg1", "yg1b", "yg2", "yg3", "yg4",
    "b", "rr1", "rr2a", "rr2b", "rr3", "rr4", "fin",
)
ORDER = (
    0, 64, 96, 2, 32, 128, 66, 160, 8, 98, 192, 34, 130, 224, 256, 257, 72, 162, 194, 136, 40, 288, 104, 226, 289, 10,
    290, 259, 42, 258, 320, 168, 200, 291, 321, 74, 232, 138, 106, 322, 356, 296, 323, 297, 420, 357, 265, 359, 170,
    202, 234, 421, 264, 389, 267, 298, 266, 299, 388, 453, 485, 358, 329, 328, 330, 391, 452, 390, 484, 423, 422, 331,
    365, 364, 516, 397, 455, 487, 454, 396, 486, 428, 429, 548, 367, 366, 518, 398, 461, 612, 550, 460, 399, 492, 493,
    431, 430, 580, 524, 556, 557, 644, 588, 462, 494, 463, 495, 614, 582, 620, 589, 526, 652, 676, 590, 653, 621, 591,
    559, 558, 684, 622, 646, 623, 654, 685, 655, 708, 686, 678, 687, 716,
)


def hadamard_signs(length):
    index = np.arange(length)
    signs = np.ones((length, length), np.float32)
    level = 1
    while level < length:
        bit_set = index // level % 2
        signs = signs * (1.0 - 2.0 * (bit_set[:, None] * bit_set[None, :]))
        level = level * 2
    return signs


def gelu_parts(pre_act):
    factor = math.sqrt(2.0 / math.pi)
    tangent = jnp.tanh(factor * (pre_act + 0.044715 * pre_act * pre_act * pre_act))
    values = 0.5 * pre_act * (1.0 + tangent)
    slopes = 0.5 * (1.0 + tangent) + 0.5 * pre_act * (1.0 - tangent * tangent) * factor * (
        1.0 + 3.0 * 0.044715 * pre_act * pre_act
    )
    return (values, slopes)


def blocks_down(v):
    return jnp.concatenate([v[:, b * HB : (b + 1) * HB] for b in range(v.shape[1] // HB)], axis=0)


def blocks_back(v, rows):
    return jnp.concatenate([v[b * rows : (b + 1) * rows] for b in range(v.shape[0] // rows)], axis=1)


def turn(v, signs):
    return jnp.dot(v, signs, preferred_element_type=F32)


def pair_scratch(n):
    _, t, tiles, out_tiles = PAIRS[n]
    wide = W // tiles
    shapes = dict(
        x=pltpu.VMEM((2, 8 * t, W), BF),
        act=pltpu.VMEM((2, 2, tiles, 8 * t, wide), BF),
        slope=pltpu.VMEM((tiles, 2 * t, wide), F32),
        out=pltpu.VMEM((t, W), BF),
        inn=pltpu.VMEM((t, W), BF),
        ss=pltpu.VMEM((2, tiles, 8 * t, wide), BF),
        sr=pltpu.VMEM((2, tiles, 8 * t, wide), BF),
        c=pltpu.VMEM((2, tiles, 8 * t, wide), BF),
        ra=pltpu.VMEM((2, tiles, 2, t, wide), BF),
        rb=pltpu.VMEM((2, tiles, 2, 2 * t, wide), BF),
    )
    for slot, number in enumerate(out_tiles):
        wide = W // number
        shapes[f"p{slot}"] = pltpu.VMEM((number, 8 * t, wide), BF)
        shapes[f"rx{slot}"] = pltpu.VMEM((number, 2, t, wide), BF)
        shapes[f"rza{slot}"] = pltpu.VMEM((number, 2, t, wide), BF)
        shapes[f"rzb{slot}"] = pltpu.VMEM((number, 2, t, wide), BF)
        shapes[f"rh{slot}"] = pltpu.VMEM((number, t, wide), BF)
    return {f"{name}_{n}": shape for name, shape in shapes.items()}


def kernel(scratch_names, *refs):
    tok, cot, w1h, b_in, w2h, b_out, signs_ref, came, stayed = refs[:9]
    named = dict(zip(scratch_names, refs[9:], strict=True))
    w1, w2, w_sem, send, recv = (named[n] for n in ("w1", "w2", "w_sem", "send", "recv"))

    s, r, col = lax.axis_index("section"), lax.axis_index("row"), lax.axis_index("col")
    z, x, y, k = lax.div(r, 2), lax.rem(r, 2), lax.div(col, 2), lax.rem(col, 2)

    def row_id(dz, dx):
        return lax.rem(z + (dz + 4), 4) * 2 + (1 - x if dx else x)

    yp, ym, yo = lax.rem(y + 1, 4), lax.rem(y + 3, 4), lax.rem(y + 2, 4)
    to = {
        "z+": {"row": row_id(1, 0)},
        "z-": {"row": row_id(-1, 0)},
        "x": {"row": row_id(0, 1)},
        "y+": {"col": yp * 2 + k},
        "y-": {"col": ym * 2 + k},
        "k": {"col": y * 2 + 1 - k},
        "s": {"section": 1 - s},
    }

    indices, copies, pending = {}, {}, []

    def remote(name, src, dst, target):
        i = indices.setdefault(name, len(indices))
        assert i < SEMAPHORES
        return pltpu.make_async_remote_copy(
            src_ref=src,
            dst_ref=dst,
            send_sem=send.at[i],
            recv_sem=recv.at[i],
            device_id=to[target],
            device_id_type=pl.DeviceIdType.MESH,
        )

    def go(name, src, dst, target):
        copies[name] = remote(name, src, dst, target)
        copies[name].start()
        pending.append(copies[name])

    def got(*names):
        for name in names:
            if name in copies:
                copies.pop(name).wait_recv()

    loads = {}

    def load_weights(which, half):
        at = pl.multiple_of((k if half == 0 else 1 - k) * W, W)
        sem = w_sem.at[2 * (which - 1) + half]
        if which == 1:
            copy = pltpu.make_async_copy(w1h.at[0, :, pl.ds(at, W)], w1.at[half], sem)
        else:
            copy = pltpu.make_async_copy(w2h.at[0, pl.ds(at, W), :], w2.at[half], sem)
        copy.start()
        loads[which, half] = copy

    def need(which, half):
        copy = loads.pop((which, half), None)
        if copy is not None:
            copy.wait()

    def rows(index, size, part=None):
        start, count = (0, size) if part is None else part
        return pl.ds(pl.multiple_of(index * size + start, 16), count)

    def add_into(buf, first, others, count):
        @pl.loop(0, count // 16)
        def _(i):
            here = pl.ds(pl.multiple_of(first + i * 16, 16), 16)
            total = buf[here, :].astype(F32)
            for other, start in others:
                there = pl.ds(pl.multiple_of(start + i * 16, 16), 16)
                total = total + other[there, :].astype(F32)
            buf[here, :] = total.astype(BF)

    class Pair:
        def __init__(self, n):
            self.n = n
            self.first, self.t, self.tiles, self.out_tiles = PAIRS[n]
            self.wide = W // self.tiles
            for name in pair_scratch(n):
                setattr(self, name[: name.rindex("_")], named[name])

        def ways(self, odd):
            t = self.t
            if t >= 32:
                h = t // 2
                return (0, h), (h, t - h), (h, t - h), (0, h)
            return (None, (0, t), (0, t), None) if odd else ((0, t), None, None, (0, t))

    class Into:
        def __init__(self, pair, kind):
            self.q, self.kind = pair, kind
            self.forward = kind == FORWARD
            self.source = (tok if self.forward else cot).at[0]
            self.x = pair.x.at[kind]
            self.tag = f"i{pair.n}{kind}"
            self.up, self.up_rest, self.down, self.down_rest = pair.ways(not self.forward)

        def go(self, name, src, dst, target):
            go(self.tag + name, src, dst, target)

        def got(self, *names):
            got(*(self.tag + name for name in names))

        def part(self, p):
            return self.source.at[pl.ds(self.q.first + p[0], p[1])]

        def give(self, name, p, target):
            if p is not None:
                self.go(name, self.part(p), self.x.at[rows(row_id(0, 0), self.q.t, p)], target)

        def ag1(self, _):
            t = self.q.t
            self.give("x0", (0, t), "x")
            self.give("zpk", self.up, "z+")
            self.give("zmk", self.down, "z-")
            i = indices.setdefault(self.tag + "own", len(indices))
            self.own = pltpu.make_async_copy(
                self.part((0, t)), self.x.at[rows(row_id(0, 0), t)], send.at[i]
            )
            self.own.start()

        def ag1b(self, _):
            self.give("zpo", self.up_rest, "z+")
            self.give("zmo", self.down_rest, "z-")

        def pass_on(self, name, at, target):
            self.go(name, self.x.at[at], self.x.at[at], target)

        def ag2a(self, _):
            t = self.q.t
            if self.up is not None:
                self.got("zpk")
                self.pass_on("fp", rows(row_id(-1, 0), t, self.up), "z+")
            if self.down is not None:
                self.got("zmk")
                self.pass_on("fm", rows(row_id(1, 0), t, self.down), "z-")

        def ag2b(self, _):
            self.got("x0")
            peer = rows(row_id(0, 1), self.q.t)
            self.pass_on("zxp", peer, "z+")
            self.pass_on("zxm", peer, "z-")

        def ag3(self, _):
            self.got("fp", "fm")
            self.pass_on("x3", rows(row_id(2, 0), self.q.t), "x")

        def ag4(self, _):
            self.own.wait()
            self.got("zpo", "zmo", "zxp", "zxm", "x3")

        def into_hidden(self, half, tile, done):
            wide = self.q.wide
            for at in range(tile * wide, (tile + 1) * wide, TN):
                cols = pl.ds(at, TN)
                if self.forward:
                    value = jnp.dot(self.x[...], w1[half, :, cols], preferred_element_type=F32)
                else:
                    value = lax.dot_general(
                        self.x[...],
                        w2[half, cols, :],
                        (((1,), (1,)), ((), ())),
                        preferred_element_type=F32,
                    )
                done(pl.ds(at - tile * wide, TN), value)

        def a1(self, _):
            need(1 if self.forward else 2, 1)
            for tile in range(self.q.tiles):
                ss, sr = self.q.ss.at[self.kind, tile], self.q.sr.at[self.kind, tile]

                def done(cols, value):
                    ss[:, cols] = value.astype(BF)

                self.into_hidden(1, tile, done)
                self.go(f"ks{tile}", ss, sr, "k")

        def a2(self, _):
            need(1 if self.forward else 2, 0)
            t, size = self.q.t, 2 * self.q.t
            h0, h1 = (0, t), (t, t)
            for tile in range(self.q.tiles):
                c, sr = self.q.c.at[self.kind, tile], self.q.sr.at[self.kind, tile]
                ra = self.q.ra.at[self.kind, tile]
                self.got(f"ks{tile}")

                def done(cols, value):
                    c[:, cols] = (value + sr[:, cols].astype(F32)).astype(BF)

                self.into_hidden(0, tile, done)
                self.go(f"rap{tile}", c.at[rows(yo, size, h0)], ra.at[0], "y+")
                self.go(f"ram{tile}", c.at[rows(yo, size, h1)], ra.at[1], "y-")

        def rs1(self, tile):
            t, size = self.q.t, 2 * self.q.t
            c, rb = self.q.c.at[self.kind, tile], self.q.rb.at[self.kind, tile]
            self.go(f"rbpe{tile}", c.at[rows(yp, size, (t, t))], rb.at[0, pl.ds(t, t)], "y+")
            self.go(f"rbme{tile}", c.at[rows(ym, size, (0, t))], rb.at[1, pl.ds(0, t)], "y-")

        def rs2(self, tile):
            t, size = self.q.t, 2 * self.q.t
            c = self.q.c.at[self.kind, tile]
            ra, rb = self.q.ra.at[self.kind, tile], self.q.rb.at[self.kind, tile]
            self.got(f"rap{tile}")
            add_into(c, yp * size, [(ra.at[0], 0)], t)
            self.go(f"rbp{tile}", c.at[rows(yp, size, (0, t))], rb.at[0, pl.ds(0, t)], "y+")
            self.got(f"ram{tile}")
            add_into(c, ym * size + t, [(ra.at[1], 0)], t)
            self.go(f"rbm{tile}", c.at[rows(ym, size, (t, t))], rb.at[1, pl.ds(t, t)], "y-")

        def rs3(self, tile):
            size, wide = 2 * self.q.t, self.q.wide
            c, rb = self.q.c.at[self.kind, tile], self.q.rb.at[self.kind, tile]
            act, slope = self.q.act.at[self.kind, 0, tile], self.q.slope.at[tile]
            self.got(*(f"{name}{tile}" for name in ("rbpe", "rbme", "rbp", "rbm")))

            @pl.loop(0, size // 16)
            def _(i):
                here = pl.ds(pl.multiple_of(y * size + i * 16, 16), 16)
                piece = pl.ds(pl.multiple_of(i * 16, 16), 16)
                total = (
                    c[here, :].astype(F32) + rb[0, piece, :].astype(F32) + rb[1, piece, :].astype(F32)
                )
                if self.forward:
                    bias = b_in[:, pl.ds(pl.multiple_of(k * W + tile * wide, wide), wide)]
                    values, slopes = gelu_parts(total + bias)
                    slope[piece, :] = slopes
                else:
                    values = total * slope[piece, :]
                act[here, :] = values.astype(BF)

    class Out:
        def __init__(self, pair, slot):
            self.q, self.slot = pair, slot
            self.kind = s if slot == GOES else 1 - s
            self.act = pair.act.at[self.kind]
            self.number = pair.out_tiles[slot]
            self.wide = W // self.number
            self.p, self.rx, self.rza, self.rzb, self.rh = (
                getattr(pair, f"{name}{slot}") for name in ("p", "rx", "rza", "rzb", "rh")
            )
            self.tag = f"o{pair.n}{slot}"
            self.up, self.up_rest, self.down, self.down_rest = pair.ways(slot)

        def go(self, name, src, dst, target):
            go(self.tag + name, src, dst, target)

        def got(self, *names):
            got(*(self.tag + name for name in names))

        def yg1(self, tile):
            t, size = self.q.t, 2 * self.q.t
            h0, h1 = rows(y, size, (0, t)), rows(y, size, (t, t))
            self.pass_on(f"gp0{tile}", tile, h0, "y+")
            self.pass_on(f"gm1{tile}", tile, h1, "y-")

        def yg1b(self, tile):
            t, size = self.q.t, 2 * self.q.t
            h0, h1 = rows(y, size, (0, t)), rows(y, size, (t, t))
            self.pass_on(f"gp1{tile}", tile, h1, "y+")
            self.pass_on(f"gm0{tile}", tile, h0, "y-")
            self.across(f"k0{tile}", tile, rows(y, size))

        def pass_on(self, name, tile, at, target):
            mine = self.act.at[0, tile, at]
            self.go(name, mine, mine, target)

        def across(self, name, tile, at):
            self.go(name, self.act.at[0, tile, at], self.act.at[1, tile, at], "k")

        def yg2(self, tile):
            t, size = self.q.t, 2 * self.q.t
            self.got(f"gp0{tile}")
            self.pass_on(f"hp{tile}", tile, rows(ym, size, (0, t)), "y+")
            self.got(f"gm1{tile}")
            self.pass_on(f"hm{tile}", tile, rows(yp, size, (t, t)), "y-")

        def yg3(self, tile):
            size = 2 * self.q.t
            self.got(f"gp1{tile}")
            self.across(f"k1{tile}", tile, rows(ym, size))
            self.got(f"gm0{tile}")
            self.across(f"k2{tile}", tile, rows(yp, size))

        def yg4(self, tile):
            t, size = self.q.t, 2 * self.q.t
            self.got(f"hp{tile}")
            self.across(f"k3{tile}", tile, rows(yo, size, (0, t)))
            self.got(f"hm{tile}")
            self.across(f"k4{tile}", tile, rows(yo, size, (t, t)))

        def product(self, kind, half, at):
            cols, wide = pl.ds(at, TN), self.q.wide
            total = None
            for tile in range(self.q.tiles):
                hidden = pl.ds(tile * wide, wide)
                if kind == FORWARD:
                    value = jnp.dot(
                        self.act[half, tile], w2[half, hidden, cols], preferred_element_type=F32
                    )
                else:
                    value = lax.dot_general(
                        self.act[half, tile],
                        w1[half, cols, hidden],
                        (((1,), (1,)), ((), ())),
                        preferred_element_type=F32,
                    )
                total = value if total is None else total + value
            return total

        def b(self, _):
            for which in (1, 2):
                for half in (0, 1):
                    need(which, half)
            for tile in range(self.q.tiles):
                self.got(*(f"k{i}{tile}" for i in range(5)))
            for out in range(self.number):
                p = self.p.at[out]

                def tile_of(kind):
                    for at in range(out * self.wide, (out + 1) * self.wide, TN):
                        total = self.product(kind, 0, at) + self.product(kind, 1, at)
                        p[:, pl.ds(at - out * self.wide, TN)] = total.astype(BF)

                pl.when(self.kind == FORWARD)(functools.partial(tile_of, FORWARD))
                pl.when(self.kind == BACKWARD)(functools.partial(tile_of, BACKWARD))
                t = self.q.t
                self.go(f"x1{out}", p.at[rows(row_id(2, 1), t)], self.rx.at[out, 0], "x")
                self.go(f"zap{out}", p.at[rows(row_id(1, 1), t)], self.rza.at[out, 0], "z+")
                self.go(f"zam{out}", p.at[rows(row_id(-1, 1), t)], self.rza.at[out, 1], "z-")

        def rr1(self, out):
            self.give_sum(f"zbpe{out}", out, row_id(1, 0), self.up_rest, 0, "z+")
            self.give_sum(f"zbme{out}", out, row_id(-1, 0), self.down_rest, 1, "z-")

        def give_sum(self, name, out, row, part, side, target):
            if part is not None:
                self.go(
                    name,
                    self.p.at[out, rows(row, self.q.t, part)],
                    self.rzb.at[out, side, pl.ds(*part)],
                    target,
                )

        def rr2a(self, out):
            t, p, far = self.q.t, self.p.at[out], row_id(2, 0)
            self.got(f"x1{out}")
            add_into(p, far * t, [(self.rx.at[out, 0], 0)], t)
            for name, part, target in (("zhp", self.up, "z+"), ("zhm", self.down, "z-")):
                if part is not None:
                    self.go(f"{name}{out}", p.at[rows(far, t, part)], self.rh.at[out, pl.ds(*part)], target)

        def rr2b(self, out):
            t, p, peer = self.q.t, self.p.at[out], row_id(0, 1)
            self.got(f"zap{out}", f"zam{out}")
            add_into(p, peer * t, [(self.rza.at[out, 0], 0), (self.rza.at[out, 1], 0)], t)
            self.go(f"x2{out}", p.at[rows(peer, t)], self.rx.at[out, 1], "x")

        def rr3(self, out):
            t, p, rh = self.q.t, self.p.at[out], self.rh.at[out]
            if self.up is not None:
                self.got(f"zhp{out}")
                add_into(p, row_id(1, 0) * t + self.up[0], [(rh, self.up[0])], self.up[1])
                self.give_sum(f"zbp{out}", out, row_id(1, 0), self.up, 0, "z+")
            if self.down is not None:
                self.got(f"zhm{out}")
                add_into(p, row_id(-1, 0) * t + self.down[0], [(rh, self.down[0])], self.down[1])
                self.give_sum(f"zbm{out}", out, row_id(-1, 0), self.down, 1, "z-")

        def rr4(self, out):
            t, wide = self.q.t, self.wide
            self.got(*(f"{name}{out}" for name in ("zbpe", "zbme", "zbp", "zbm", "x2")))
            mine = rows(row_id(0, 0), t)
            cols = pl.ds(out * wide, wide)
            total = (
                self.p[out, mine, :].astype(F32)
                + self.rzb[out, 0].astype(F32)
                + self.rzb[out, 1].astype(F32)
                + self.rx[out, 1].astype(F32)
                + self.q.x[self.kind, mine, cols].astype(F32)
            )
            total = total + jnp.where(self.kind == FORWARD, b_out[:, cols], 0.0)
            if self.slot == STAYS:
                stayed[pl.ds(self.q.first, t), cols] = total.astype(BF)
                return
            stacked = blocks_down(total)
            high = stacked.astype(BF)
            rest = stacked - high.astype(F32)
            mid = rest.astype(BF)
            low = (rest - mid.astype(F32)).astype(BF)
            signs = signs_ref[...]
            turned = turn(high, signs) + (turn(mid, signs) + turn(low, signs))
            turned = turned * (1.0 / math.sqrt(HB))
            self.q.out[:, cols] = blocks_back(turned, t).astype(BF)
            self.go(f"sec{out}", self.q.out.at[:, cols], self.q.inn.at[:, cols], "s")

        def fin(self, _):
            self.got(*(f"sec{out}" for out in range(self.number)))
            came[pl.ds(self.q.first, self.q.t), :] = self.q.inn[...]

    for which, half in ((1, 1), (1, 0), (2, 1), (2, 0)):
        load_weights(which, half)

    barrier = pltpu.get_barrier_semaphore()
    for target in to.values():
        pl.semaphore_signal(barrier, inc=1, device_id=target, device_id_type=pl.DeviceIdType.MESH)
    pl.semaphore_wait(barrier, len(to))

    jobs = []
    for n in range(len(PAIRS)):
        pair = Pair(n)
        jobs.append((Into(pair, FORWARD), Into(pair, BACKWARD), Out(pair, GOES), Out(pair, STAYS)))
    for step in ORDER:
        phase, job = PHASES[step // 32], jobs[step // 8 % 4][step // 2 % 4]
        getattr(job, phase)(step % 2)
    for copy in pending:
        copy.wait_send()


def finish_kernel(came, stayed, signs, handed, leaving):
    turned = turn(blocks_down(came[...]), signs[...]) * (1.0 / math.sqrt(HB))
    handed[0] = blocks_back(turned, came.shape[0])
    leaving[0] = stayed[...]


def on_device(tokens, cotangent, w_in, b_in, w_out, b_out):
    scratch = dict(
        w1=pltpu.VMEM((2, W, W), BF),
        w2=pltpu.VMEM((2, W, W), BF),
        w_sem=pltpu.SemaphoreType.DMA((4,)),
        send=pltpu.SemaphoreType.DMA((SEMAPHORES,)),
        recv=pltpu.SemaphoreType.DMA((SEMAPHORES,)),
    )
    for n in range(len(PAIRS)):
        scratch.update(pair_scratch(n))
    signs = jnp.asarray(hadamard_signs(HB), BF)
    vmem, anywhere = pl.BlockSpec(memory_space=pltpu.VMEM), pl.BlockSpec(memory_space=pl.ANY)
    tile = jax.ShapeDtypeStruct(tokens.shape[1:], BF)
    came, stayed = pl.pallas_call(
        functools.partial(kernel, tuple(scratch)),
        out_shape=(tile, tile),
        in_specs=[anywhere, anywhere, anywhere, vmem, anywhere, vmem, vmem],
        out_specs=(vmem, vmem),
        scratch_shapes=list(scratch.values()),
        cost_estimate=pl.CostEstimate(flops=19_500_000_000, bytes_accessed=20_000_000, transcendentals=200_000),
        compiler_params=pltpu.CompilerParams(
            collective_id=0, has_side_effects=True, vmem_limit_bytes=56 << 20
        ),
        name="feed_forward",
    )(tokens, cotangent, w_in, b_in, w_out, b_out, signs)
    return pl.pallas_call(
        finish_kernel,
        out_shape=(
            jax.ShapeDtypeStruct(tokens.shape, F32),
            jax.ShapeDtypeStruct(tokens.shape, BF),
        ),
        in_specs=[vmem, vmem, vmem],
        out_specs=(vmem, vmem),
        name="hand_over",
    )(came, stayed, signs)


def solution(mesh):
    in_specs = (
        P("section", "row", "col"),
        P("section", "row", "col"),
        P("section", "col", "row"),
        P("section", "row"),
        P("section", "row", "col"),
        P("section", "col"),
    )
    out_specs = (P("section", "row", "col"), P("section", "row", "col"))
    return jax.shard_map(
        on_device, mesh=mesh, in_specs=in_specs, out_specs=out_specs, check_vma=False
    )
```

```python
import functools
import math

import jax
import jax.numpy as jnp
import numpy as np
from jax import lax
from jax.experimental import pallas as pl
from jax.experimental.pallas import tpu as pltpu
from jax.sharding import PartitionSpec as P

HB = 128
W = 1536
TN = 768
BF = jnp.bfloat16
F32 = jnp.float32


PAIRS = ((0, 32, 2, (1, 1), True, (False, False)), (32, 32, 1, (2, 2), False, (True, True)))
FORWARD, BACKWARD = 0, 1
GOES, STAYS = 0, 1
SEMAPHORES = 320

PHASES = (
    "ag1", "ag1b", "ag2a", "ag2b", "ag3", "ag4", "a1", "a2", "rs1", "rs2", "rs3", "yg1", "yg1b", "yg2", "yg3", "yg4",
    "b", "rr1", "rr2a", "rr2b", "rr3", "rr4", "fin",
)
ORDER = (
    0, 64, 32, 2, 128, 66, 96, 34, 98, 130, 10, 160, 193, 192, 225, 224, 162, 195, 256, 8, 257, 74, 42, 227, 259, 106,
    288, 194, 289, 138, 72, 291, 226, 258, 321, 40, 323, 357, 359, 104, 320, 136, 170, 391, 389, 202, 290, 421, 234,
    266, 168, 200, 322, 356, 453, 485, 358, 232, 420, 388, 264, 296, 298, 452, 423, 484, 390, 455, 422, 516, 328, 330,
    364, 396, 487, 454, 486, 580, 612, 548, 428, 366, 518, 460, 492, 398, 644, 550, 524, 430, 582, 556, 525, 557, 462,
    614, 676, 494, 620, 646, 588, 652, 526, 621, 589, 527, 653, 708, 558, 622, 590, 678, 684, 685, 591, 623, 559, 654,
    686, 716, 655, 687,
)


def hadamard_signs(length):
    index = np.arange(length)
    signs = np.ones((length, length), np.float32)
    level = 1
    while level < length:
        bit_set = index // level % 2
        signs = signs * (1.0 - 2.0 * (bit_set[:, None] * bit_set[None, :]))
        level = level * 2
    return signs


def gelu_parts(pre_act):
    factor = math.sqrt(2.0 / math.pi)
    tangent = jnp.tanh(factor * (pre_act + 0.044715 * pre_act * pre_act * pre_act))
    values = 0.5 * pre_act * (1.0 + tangent)
    slopes = 0.5 * (1.0 + tangent) + 0.5 * pre_act * (1.0 - tangent * tangent) * factor * (
        1.0 + 3.0 * 0.044715 * pre_act * pre_act
    )
    return (values, slopes)


def blocks_down(v):
    return jnp.concatenate([v[:, b * HB : (b + 1) * HB] for b in range(v.shape[1] // HB)], axis=0)


def blocks_back(v, rows):
    return jnp.concatenate([v[b * rows : (b + 1) * rows] for b in range(v.shape[0] // rows)], axis=1)


def turn(v, signs):
    return jnp.dot(v, signs, preferred_element_type=F32)


def pair_scratch(n):
    _, t, tiles, out_tiles, _, _ = PAIRS[n]
    wide = W // tiles
    shapes = dict(
        x=pltpu.VMEM((2, 8 * t, W), BF),
        act=pltpu.VMEM((2, 2, tiles, 8 * t, wide), BF),
        slope=pltpu.VMEM((tiles, 2 * t, wide), F32),
        out=pltpu.VMEM((t, W), BF),
        inn=pltpu.VMEM((t, W), BF),
        ss=pltpu.VMEM((2, tiles, 8 * t, wide), BF),
        sr=pltpu.VMEM((2, tiles, 8 * t, wide), BF),
        c=pltpu.VMEM((2, tiles, 8 * t, wide), BF),
        ra=pltpu.VMEM((2, tiles, 2, t, wide), BF),
        rb=pltpu.VMEM((2, tiles, 2, 2 * t, wide), BF),
    )
    for slot, number in enumerate(out_tiles):
        wide = W // number
        shapes[f"p{slot}"] = pltpu.VMEM((number, 8 * t, wide), BF)
        shapes[f"rx{slot}"] = pltpu.VMEM((number, 2, t, wide), BF)
        shapes[f"rza{slot}"] = pltpu.VMEM((number, 2, t, wide), BF)
        shapes[f"rzb{slot}"] = pltpu.VMEM((number, 2, t, wide), BF)
        shapes[f"rh{slot}"] = pltpu.VMEM((number, t, wide), BF)
    return {f"{name}_{n}": shape for name, shape in shapes.items()}


def kernel(scratch_names, *refs):
    tok, cot, w1h, b_in, w2h, b_out, signs_ref, came, stayed = refs[:9]
    named = dict(zip(scratch_names, refs[9:], strict=True))
    w1, w2, w_sem, send, recv = (named[n] for n in ("w1", "w2", "w_sem", "send", "recv"))

    s, r, col = lax.axis_index("section"), lax.axis_index("row"), lax.axis_index("col")
    z, x, y, k = lax.div(r, 2), lax.rem(r, 2), lax.div(col, 2), lax.rem(col, 2)

    row_ids = {}
    for dz in (0, 1, -1, 2):
        for dx in (0, 1):
            row_ids[dz, dx] = lax.rem(z + (dz + 4), 4) * 2 + (1 - x if dx else x)

    def row_id(dz, dx):
        return row_ids[dz, dx]

    yp, ym, yo = lax.rem(y + 1, 4), lax.rem(y + 3, 4), lax.rem(y + 2, 4)
    to = {
        "z+": (s, row_id(1, 0), col),
        "z-": (s, row_id(-1, 0), col),
        "z2": (s, row_id(2, 0), col),
        "x": (s, row_id(0, 1), col),
        "y+": (s, r, yp * 2 + k),
        "y-": (s, r, ym * 2 + k),
        "k": (s, r, y * 2 + 1 - k),
        "s": (1 - s, r, col),
    }

    indices, copies, pending = {}, {}, []

    def remote(name, src, dst, target):
        i = indices.setdefault(name, len(indices))
        assert i < SEMAPHORES
        return pltpu.make_async_remote_copy(
            src_ref=src,
            dst_ref=dst,
            send_sem=send.at[i],
            recv_sem=recv.at[i],
            device_id=to[target],
            device_id_type=pl.DeviceIdType.MESH,
        )

    def go(name, src, dst, target):
        copies[name] = remote(name, src, dst, target)
        copies[name].start()
        pending.append(copies[name])

    def got(*names):
        for name in names:
            if name in copies:
                copies.pop(name).wait_recv()

    def settle(keep):
        sent = pending[: max(0, len(pending) - keep)]
        del pending[: len(sent)]
        for copy in sent:
            copy.wait_send()

    loads = {}

    def load_weights(which, half):
        at = pl.multiple_of((k if half == 0 else 1 - k) * W, W)
        sem = w_sem.at[2 * (which - 1) + half]
        if which == 1:
            copy = pltpu.make_async_copy(w1h.at[0, :, pl.ds(at, W)], w1.at[half], sem)
        else:
            copy = pltpu.make_async_copy(w2h.at[0, pl.ds(at, W), :], w2.at[half], sem)
        copy.start()
        loads[which, half] = copy

    def need(which, half):
        copy = loads.pop((which, half), None)
        if copy is not None:
            copy.wait()

    def rows(index, size, part=None):
        start, count = (0, size) if part is None else part
        return pl.ds(pl.multiple_of(index * size + start, 16), count)

    def add_into(buf, first, others, count):
        @pl.loop(0, count // 16)
        def _(i):
            here = pl.ds(pl.multiple_of(first + i * 16, 16), 16)
            total = buf[here, :].astype(F32)
            for other, start in others:
                there = pl.ds(pl.multiple_of(start + i * 16, 16), 16)
                total = total + other[there, :].astype(F32)
            buf[here, :] = total.astype(BF)

    class Pair:
        def __init__(self, n):
            self.n = n
            self.first, self.t, self.tiles, self.out_tiles, self.straight, self.out_straight = PAIRS[n]
            self.wide = W // self.tiles
            for name in pair_scratch(n):
                setattr(self, name[: name.rindex("_")], named[name])

        def ways(self, odd, straight):
            t = self.t
            if straight:
                return None, (0, t), None, (0, t)
            if t >= 32:
                h = t // 2
                return (0, h), (h, t - h), (h, t - h), (0, h)
            return (None, (0, t), (0, t), None) if odd else ((0, t), None, None, (0, t))

    class Into:
        def __init__(self, pair, kind):
            self.q, self.kind = pair, kind
            self.forward = kind == FORWARD
            self.source = (tok if self.forward else cot).at[0]
            self.x = pair.x.at[kind]
            self.tag = f"i{pair.n}{kind}"
            self.up, self.up_rest, self.down, self.down_rest = pair.ways(not self.forward, pair.straight)

        def go(self, name, src, dst, target):
            go(self.tag + name, src, dst, target)

        def got(self, *names):
            got(*(self.tag + name for name in names))

        def part(self, p):
            return self.source.at[pl.ds(self.q.first + p[0], p[1])]

        def give(self, name, p, target):
            if p is not None:
                self.go(name, self.part(p), self.x.at[rows(row_id(0, 0), self.q.t, p)], target)

        def ag1(self, _):
            t = self.q.t
            self.give("x0", (0, t), "x")
            if self.q.straight:
                self.give("z2", (0, t), "z2")
            self.give("zpk", self.up, "z+")
            self.give("zmk", self.down, "z-")
            i = indices.setdefault(self.tag + "own", len(indices))
            self.own = pltpu.make_async_copy(
                self.part((0, t)), self.x.at[rows(row_id(0, 0), t)], send.at[i]
            )
            self.own.start()

        def ag1b(self, _):
            self.give("zpo", self.up_rest, "z+")
            self.give("zmo", self.down_rest, "z-")

        def pass_on(self, name, at, target):
            self.go(name, self.x.at[at], self.x.at[at], target)

        def ag2a(self, _):
            t = self.q.t
            if self.up is not None:
                self.got("zpk")
                self.pass_on("fp", rows(row_id(-1, 0), t, self.up), "z+")
            if self.down is not None:
                self.got("zmk")
                self.pass_on("fm", rows(row_id(1, 0), t, self.down), "z-")

        def ag2b(self, _):
            self.got("x0")
            peer = rows(row_id(0, 1), self.q.t)
            self.pass_on("zxp", peer, "z+")
            self.pass_on("zxm", peer, "z-")

        def ag3(self, _):
            self.got("fp", "fm", "z2")
            self.pass_on("x3", rows(row_id(2, 0), self.q.t), "x")

        def ag4(self, _):
            self.own.wait()
            self.got("zpo", "zmo", "zxp", "zxm", "x3")

        def into_hidden(self, half, tile, done):
            wide = self.q.wide
            for at in range(tile * wide, (tile + 1) * wide, TN):
                cols = pl.ds(at, TN)
                if self.forward:
                    value = jnp.dot(self.x[...], w1[half, :, cols], preferred_element_type=F32)
                else:
                    value = lax.dot_general(
                        self.x[...],
                        w2[half, cols, :],
                        (((1,), (1,)), ((), ())),
                        preferred_element_type=F32,
                    )
                done(pl.ds(at - tile * wide, TN), value)

        def a1(self, tile):
            need(1 if self.forward else 2, 1)
            ss, sr = self.q.ss.at[self.kind, tile], self.q.sr.at[self.kind, tile]

            def done(cols, value):
                ss[:, cols] = value.astype(BF)

            self.into_hidden(1, tile, done)
            self.go(f"ks{tile}", ss, sr, "k")

        def a2(self, tile):
            need(1 if self.forward else 2, 0)
            t, size = self.q.t, 2 * self.q.t
            c, sr, ra = (buf.at[self.kind, tile] for buf in (self.q.c, self.q.sr, self.q.ra))

            def done(cols, value):
                self.got(f"ks{tile}")
                c[:, cols] = (value + sr[:, cols].astype(F32)).astype(BF)

            self.into_hidden(0, tile, done)
            self.go(f"rap{tile}", c.at[rows(yo, size, (0, t))], ra.at[0], "y+")
            self.go(f"ram{tile}", c.at[rows(yo, size, (t, t))], ra.at[1], "y-")

        def rs1(self, tile):
            t, size = self.q.t, 2 * self.q.t
            c, rb = self.q.c.at[self.kind, tile], self.q.rb.at[self.kind, tile]
            self.go(f"rbpe{tile}", c.at[rows(yp, size, (t, t))], rb.at[0, pl.ds(t, t)], "y+")
            self.go(f"rbme{tile}", c.at[rows(ym, size, (0, t))], rb.at[1, pl.ds(0, t)], "y-")

        def rs2(self, tile):
            t, size = self.q.t, 2 * self.q.t
            c = self.q.c.at[self.kind, tile]
            ra, rb = self.q.ra.at[self.kind, tile], self.q.rb.at[self.kind, tile]
            self.got(f"rap{tile}")
            add_into(c, yp * size, [(ra.at[0], 0)], t)
            self.go(f"rbp{tile}", c.at[rows(yp, size, (0, t))], rb.at[0, pl.ds(0, t)], "y+")
            self.got(f"ram{tile}")
            add_into(c, ym * size + t, [(ra.at[1], 0)], t)
            self.go(f"rbm{tile}", c.at[rows(ym, size, (t, t))], rb.at[1, pl.ds(t, t)], "y-")

        def rs3(self, tile):
            size, wide = 2 * self.q.t, self.q.wide
            c, rb = self.q.c.at[self.kind, tile], self.q.rb.at[self.kind, tile]
            act, slope = self.q.act.at[self.kind, 0, tile], self.q.slope.at[tile]
            self.got(*(f"{name}{tile}" for name in ("rbpe", "rbme", "rbp", "rbm")))

            @pl.loop(0, size // 16)
            def _(i):
                here = pl.ds(pl.multiple_of(y * size + i * 16, 16), 16)
                piece = pl.ds(pl.multiple_of(i * 16, 16), 16)
                total = (
                    c[here, :].astype(F32) + rb[0, piece, :].astype(F32) + rb[1, piece, :].astype(F32)
                )
                if self.forward:
                    bias = b_in[:, pl.ds(pl.multiple_of(k * W + tile * wide, wide), wide)]
                    values, slopes = gelu_parts(total + bias)
                    slope[piece, :] = slopes
                else:
                    values = total * slope[piece, :]
                act[here, :] = values.astype(BF)

    class Out:
        def __init__(self, pair, slot):
            self.q, self.slot = pair, slot
            self.kind = s if slot == GOES else 1 - s
            self.act = pair.act.at[self.kind]
            self.number = pair.out_tiles[slot]
            self.wide = W // self.number
            self.p, self.rx, self.rza, self.rzb, self.rh = (
                getattr(pair, f"{name}{slot}") for name in ("p", "rx", "rza", "rzb", "rh")
            )
            self.tag = f"o{pair.n}{slot}"
            self.up, self.up_rest, self.down, self.down_rest = pair.ways(slot, pair.out_straight[slot])

        def go(self, name, src, dst, target):
            go(self.tag + name, src, dst, target)

        def got(self, *names):
            got(*(self.tag + name for name in names))

        def yg1(self, tile):
            t, size = self.q.t, 2 * self.q.t
            h0, h1 = rows(y, size, (0, t)), rows(y, size, (t, t))
            self.pass_on(f"gp0{tile}", tile, h0, "y+")
            self.pass_on(f"gm1{tile}", tile, h1, "y-")

        def yg1b(self, tile):
            t, size = self.q.t, 2 * self.q.t
            h0, h1 = rows(y, size, (0, t)), rows(y, size, (t, t))
            self.pass_on(f"gp1{tile}", tile, h1, "y+")
            self.pass_on(f"gm0{tile}", tile, h0, "y-")
            self.across(f"k0{tile}", tile, rows(y, size))

        def pass_on(self, name, tile, at, target):
            mine = self.act.at[0, tile, at]
            self.go(name, mine, mine, target)

        def across(self, name, tile, at):
            self.go(name, self.act.at[0, tile, at], self.act.at[1, tile, at], "k")

        def yg2(self, tile):
            t, size = self.q.t, 2 * self.q.t
            self.got(f"gp0{tile}")
            self.pass_on(f"hp{tile}", tile, rows(ym, size, (0, t)), "y+")
            self.got(f"gm1{tile}")
            self.pass_on(f"hm{tile}", tile, rows(yp, size, (t, t)), "y-")

        def yg3(self, tile):
            size = 2 * self.q.t
            self.got(f"gp1{tile}")
            self.across(f"k1{tile}", tile, rows(ym, size))
            self.got(f"gm0{tile}")
            self.across(f"k2{tile}", tile, rows(yp, size))

        def yg4(self, tile):
            t, size = self.q.t, 2 * self.q.t
            self.got(f"hp{tile}")
            self.across(f"k3{tile}", tile, rows(yo, size, (0, t)))
            self.got(f"hm{tile}")
            self.across(f"k4{tile}", tile, rows(yo, size, (t, t)))

        def product(self, kind, half, at):
            cols, wide = pl.ds(at, TN), self.q.wide
            total = None
            for tile in range(self.q.tiles):
                hidden = pl.ds(tile * wide, wide)
                if kind == FORWARD:
                    value = jnp.dot(
                        self.act[half, tile], w2[half, hidden, cols], preferred_element_type=F32
                    )
                else:
                    value = lax.dot_general(
                        self.act[half, tile],
                        w1[half, cols, hidden],
                        (((1,), (1,)), ((), ())),
                        preferred_element_type=F32,
                    )
                total = value if total is None else total + value
            return total

        def b(self, out):
            for which in (1, 2):
                for half in (0, 1):
                    need(which, half)
            settle(30)
            waits = [copies.pop(f"{self.tag}k{i}{tile}") for tile in range(self.q.tiles) for i in range(5)] if out == 0 else []
            p, t = self.p.at[out], self.q.t

            def tile_of(kind):
                for at in range(out * self.wide, (out + 1) * self.wide, TN):
                    total = self.product(kind, 0, at)
                    if at == 0:
                        for copy in waits:
                            copy.wait_recv()
                    total = total + self.product(kind, 1, at)
                    p[:, pl.ds(at - out * self.wide, TN)] = total.astype(BF)

            pl.when(self.kind == FORWARD)(functools.partial(tile_of, FORWARD))
            pl.when(self.kind == BACKWARD)(functools.partial(tile_of, BACKWARD))
            self.go(f"x1{out}", p.at[rows(row_id(2, 1), t)], self.rx.at[out, 0], "x")
            self.go(f"zap{out}", p.at[rows(row_id(1, 1), t)], self.rza.at[out, 0], "z+")
            self.go(f"zam{out}", p.at[rows(row_id(-1, 1), t)], self.rza.at[out, 1], "z-")

        def rr1(self, out):
            self.give_sum(f"zbpe{out}", out, row_id(1, 0), self.up_rest, 0, "z+")
            self.give_sum(f"zbme{out}", out, row_id(-1, 0), self.down_rest, 1, "z-")

        def give_sum(self, name, out, row, part, side, target):
            if part is not None:
                self.go(
                    name,
                    self.p.at[out, rows(row, self.q.t, part)],
                    self.rzb.at[out, side, pl.ds(*part)],
                    target,
                )

        def rr2a(self, out):
            t, p, far = self.q.t, self.p.at[out], row_id(2, 0)
            self.got(f"x1{out}")
            add_into(p, far * t, [(self.rx.at[out, 0], 0)], t)
            for name, part, target in (("zhp", self.up, "z+"), ("zhm", self.down, "z-")):
                if part is not None:
                    self.go(f"{name}{out}", p.at[rows(far, t, part)], self.rh.at[out, pl.ds(*part)], target)
            if self.q.out_straight[self.slot]:
                self.go(f"z2{out}", p.at[rows(far, t)], self.rh.at[out], "z2")

        def rr2b(self, out):
            t, p, peer = self.q.t, self.p.at[out], row_id(0, 1)
            self.got(f"zap{out}", f"zam{out}")
            add_into(p, peer * t, [(self.rza.at[out, 0], 0), (self.rza.at[out, 1], 0)], t)
            self.go(f"x2{out}", p.at[rows(peer, t)], self.rx.at[out, 1], "x")

        def rr3(self, out):
            t, p, rh = self.q.t, self.p.at[out], self.rh.at[out]
            settle(16)
            if self.up is not None:
                self.got(f"zhp{out}")
                add_into(p, row_id(1, 0) * t + self.up[0], [(rh, self.up[0])], self.up[1])
                self.give_sum(f"zbp{out}", out, row_id(1, 0), self.up, 0, "z+")
            if self.down is not None:
                self.got(f"zhm{out}")
                add_into(p, row_id(-1, 0) * t + self.down[0], [(rh, self.down[0])], self.down[1])
                self.give_sum(f"zbm{out}", out, row_id(-1, 0), self.down, 1, "z-")

        def rr4(self, out):
            t, wide = self.q.t, self.wide
            self.got(*(f"{name}{out}" for name in ("zbpe", "zbme", "zbp", "zbm", "x2", "z2")))
            mine = rows(row_id(0, 0), t)
            cols = pl.ds(out * wide, wide)
            total = (
                self.p[out, mine, :].astype(F32)
                + self.rzb[out, 0].astype(F32)
                + self.rzb[out, 1].astype(F32)
                + self.rx[out, 1].astype(F32)
                + self.q.x[self.kind, mine, cols].astype(F32)
            )
            if self.q.out_straight[self.slot]:
                total = total + self.rh[out].astype(F32)
            total = total + jnp.where(self.kind == FORWARD, b_out[:, cols], 0.0)
            if self.slot == STAYS:
                stayed[pl.ds(self.q.first, t), cols] = total.astype(BF)
                return
            stacked = blocks_down(total)
            high = stacked.astype(BF)
            rest = stacked - high.astype(F32)
            mid = rest.astype(BF)
            low = (rest - mid.astype(F32)).astype(BF)
            signs = signs_ref[...]
            turned = turn(high, signs) + (turn(mid, signs) + turn(low, signs))
            turned = turned * (1.0 / math.sqrt(HB))
            self.q.out[:, cols] = blocks_back(turned, t).astype(BF)
            self.go(f"sec{out}", self.q.out.at[:, cols], self.q.inn.at[:, cols], "s")

        def fin(self, _):
            self.got(*(f"sec{out}" for out in range(self.number)))
            came[pl.ds(self.q.first, self.q.t), :] = self.q.inn[...]

    for which, half in ((1, 1), (1, 0), (2, 1), (2, 0)):
        load_weights(which, half)

    barrier = pltpu.get_barrier_semaphore()
    for target in to.values():
        pl.semaphore_signal(barrier, inc=1, device_id=target, device_id_type=pl.DeviceIdType.MESH)
    pl.semaphore_wait(barrier, len(to))

    jobs = []
    for n in range(len(PAIRS)):
        pair = Pair(n)
        jobs.append((Into(pair, FORWARD), Into(pair, BACKWARD), Out(pair, GOES), Out(pair, STAYS)))
    for step in ORDER:
        phase, job = PHASES[step // 32], jobs[step // 8 % 4][step // 2 % 4]
        getattr(job, phase)(step % 2)
    settle(0)


def finish_kernel(came, stayed, signs, handed, leaving):
    turned = turn(blocks_down(came[...]), signs[...]) * (1.0 / math.sqrt(HB))
    handed[0] = blocks_back(turned, came.shape[0])
    leaving[0] = stayed[...]


def on_device(tokens, cotangent, w_in, b_in, w_out, b_out):
    scratch = dict(
        w1=pltpu.VMEM((2, W, W), BF),
        w2=pltpu.VMEM((2, W, W), BF),
        w_sem=pltpu.SemaphoreType.DMA((4,)),
        send=pltpu.SemaphoreType.DMA((SEMAPHORES,)),
        recv=pltpu.SemaphoreType.DMA((SEMAPHORES,)),
    )
    for n in range(len(PAIRS)):
        scratch.update(pair_scratch(n))
    signs = jnp.asarray(hadamard_signs(HB), BF)
    vmem, anywhere = pl.BlockSpec(memory_space=pltpu.VMEM), pl.BlockSpec(memory_space=pl.ANY)
    tile = jax.ShapeDtypeStruct(tokens.shape[1:], BF)
    came, stayed = pl.pallas_call(
        functools.partial(kernel, tuple(scratch)),
        out_shape=(tile, tile),
        in_specs=[anywhere, anywhere, anywhere, vmem, anywhere, vmem, vmem],
        out_specs=(vmem, vmem),
        scratch_shapes=list(scratch.values()),
        cost_estimate=pl.CostEstimate(flops=19_500_000_000, bytes_accessed=20_000_000, transcendentals=200_000),
        compiler_params=pltpu.CompilerParams(
            collective_id=0, has_side_effects=True, vmem_limit_bytes=56 << 20
        ),
        name="feed_forward",
    )(tokens, cotangent, w_in, b_in, w_out, b_out, signs)
    return pl.pallas_call(
        finish_kernel,
        out_shape=(
            jax.ShapeDtypeStruct(tokens.shape, F32),
            jax.ShapeDtypeStruct(tokens.shape, BF),
        ),
        in_specs=[vmem, vmem, vmem],
        out_specs=(vmem, vmem),
        name="hand_over",
    )(came, stayed, signs)


def solution(mesh):
    in_specs = (
        P("section", "row", "col"),
        P("section", "row", "col"),
        P("section", "col", "row"),
        P("section", "row"),
        P("section", "row", "col"),
        P("section", "col"),
    )
    out_specs = (P("section", "row", "col"), P("section", "row", "col"))
    return jax.shard_map(
        on_device, mesh=mesh, in_specs=in_specs, out_specs=out_specs, check_vma=False
    )
```

```python
import functools
import math

import jax
import jax.numpy as jnp
import numpy as np
from jax import lax
from jax.experimental import pallas as pl
from jax.experimental.pallas import tpu as pltpu
from jax.sharding import PartitionSpec as P

HB = 128
W = 1536
TN = 768
BF = jnp.bfloat16
F32 = jnp.float32


PAIRS = ((0, 32, 2, (1, 1), True, (False, False)), (32, 32, 1, (2, 2), False, (True, True)))
FORWARD, BACKWARD = 0, 1
GOES, STAYS = 0, 1
SEMAPHORES = 320

PHASES = (
    "ag1", "ag1b", "ag2a", "ag2b", "ag3", "ag4", "a1", "a2", "rs1", "rs2", "rs3", "yg1", "yg1b", "yg2", "yg3", "yg4",
    "b", "rr1", "rr2a", "rr2b", "rr3", "rr4", "fin",
)
ORDER = (
    0, 64, 32, 2, 96, 128, 34, 98, 8, 40, 66, 130, 160, 192, 193, 224, 256, 225, 162, 194, 72, 257, 195, 288, 226,
    258, 10, 42, 227, 259, 136, 104, 290, 74, 289, 320, 291, 106, 322, 356, 388, 358, 168, 321, 390, 138, 200, 323,
    359, 420, 357, 389, 232, 264, 170, 202, 234, 421, 296, 266, 298, 452, 422, 391, 453, 485, 484, 516, 423, 328, 330,
    364, 396, 454, 486, 455, 487, 612, 580, 428, 366, 398, 548, 518, 460, 492, 550, 644, 430, 524, 556, 525, 462, 557,
    494, 582, 588, 620, 526, 589, 621, 527, 558, 653, 676, 590, 654, 652, 622, 646, 684, 614, 685, 591, 559, 623, 686,
    678, 708, 716, 655, 687,
)


def hadamard_signs(length):
    index = np.arange(length)
    signs = np.ones((length, length), np.float32)
    level = 1
    while level < length:
        bit_set = index // level % 2
        signs = signs * (1.0 - 2.0 * (bit_set[:, None] * bit_set[None, :]))
        level = level * 2
    return signs


def gelu_parts(pre_act):
    factor = math.sqrt(2.0 / math.pi)
    tangent = jnp.tanh(factor * (pre_act + 0.044715 * pre_act * pre_act * pre_act))
    values = 0.5 * pre_act * (1.0 + tangent)
    slopes = 0.5 * (1.0 + tangent) + 0.5 * pre_act * (1.0 - tangent * tangent) * factor * (
        1.0 + 3.0 * 0.044715 * pre_act * pre_act
    )
    return (values, slopes)


def blocks_down(v):
    return jnp.concatenate([v[:, b * HB : (b + 1) * HB] for b in range(v.shape[1] // HB)], axis=0)


def blocks_back(v, rows):
    return jnp.concatenate([v[b * rows : (b + 1) * rows] for b in range(v.shape[0] // rows)], axis=1)


def turn(v, signs):
    return jnp.dot(v, signs, preferred_element_type=F32)


def pair_scratch(n):
    _, t, tiles, out_tiles, _, _ = PAIRS[n]
    wide = W // tiles
    shapes = dict(
        x=pltpu.VMEM((2, 8 * t, W), BF),
        act=pltpu.VMEM((2, 2, tiles, 8 * t, wide), BF),
        slope=pltpu.VMEM((tiles, 2 * t, wide), F32),
        out=pltpu.VMEM((t, W), BF),
        inn=pltpu.VMEM((t, W), BF),
        ss=pltpu.VMEM((2, tiles, 8 * t, wide), BF),
        sr=pltpu.VMEM((2, tiles, 8 * t, wide), BF),
        c=pltpu.VMEM((2, tiles, 8 * t, wide), BF),
        ra=pltpu.VMEM((2, tiles, 2, t, wide), BF),
        rb=pltpu.VMEM((2, tiles, 2, 2 * t, wide), BF),
    )
    for slot, number in enumerate(out_tiles):
        wide = W // number
        shapes[f"p{slot}"] = pltpu.VMEM((number, 8 * t, wide), BF)
        shapes[f"rx{slot}"] = pltpu.VMEM((number, 2, t, wide), BF)
        shapes[f"rza{slot}"] = pltpu.VMEM((number, 2, t, wide), BF)
        shapes[f"rzb{slot}"] = pltpu.VMEM((number, 2, t, wide), BF)
        shapes[f"rh{slot}"] = pltpu.VMEM((number, t, wide), BF)
    return {f"{name}_{n}": shape for name, shape in shapes.items()}


def kernel(scratch_names, *refs):
    tok, cot, w1h, b_in_h, w2h, b_out_h, signs_h, came, stayed = refs[:9]
    named = dict(zip(scratch_names, refs[9:], strict=True))
    w1, w2, w_sem, send, recv = (named[n] for n in ("w1", "w2", "w_sem", "send", "recv"))
    b_in, b_out, signs_ref = named["b_in"], named["b_out"], named["signs"]

    s, r, col = lax.axis_index("section"), lax.axis_index("row"), lax.axis_index("col")
    z, x, y, k = lax.div(r, 2), lax.rem(r, 2), lax.div(col, 2), lax.rem(col, 2)

    row_ids = {}
    for dz in (0, 1, -1, 2):
        for dx in (0, 1):
            row_ids[dz, dx] = lax.rem(z + (dz + 4), 4) * 2 + (1 - x if dx else x)

    def row_id(dz, dx):
        return row_ids[dz, dx]

    yp, ym, yo = lax.rem(y + 1, 4), lax.rem(y + 3, 4), lax.rem(y + 2, 4)
    to = {
        "z+": (s, row_id(1, 0), col),
        "z-": (s, row_id(-1, 0), col),
        "z2": (s, row_id(2, 0), col),
        "x": (s, row_id(0, 1), col),
        "y+": (s, r, yp * 2 + k),
        "y-": (s, r, ym * 2 + k),
        "k": (s, r, y * 2 + 1 - k),
        "s": (1 - s, r, col),
    }

    indices, copies, pending = {}, {}, []

    def remote(name, src, dst, target):
        i = indices.setdefault(name, len(indices))
        assert i < SEMAPHORES
        return pltpu.make_async_remote_copy(
            src_ref=src,
            dst_ref=dst,
            send_sem=send.at[i],
            recv_sem=recv.at[i],
            device_id=to[target],
            device_id_type=pl.DeviceIdType.MESH,
        )

    def go(name, src, dst, target):
        copies[name] = remote(name, src, dst, target)
        copies[name].start()
        pending.append(copies[name])

    def got(*names):
        for name in names:
            if name in copies:
                copies.pop(name).wait_recv()

    def settle(keep):
        sent = pending[: max(0, len(pending) - keep)]
        del pending[: len(sent)]
        for copy in sent:
            copy.wait_send()

    loads = {}

    def load_weights(which, half):
        at = pl.multiple_of((k if half == 0 else 1 - k) * W, W)
        sem = w_sem.at[2 * (which - 1) + half]
        if which == 1:
            copy = pltpu.make_async_copy(w1h.at[0, :, pl.ds(at, W)], w1.at[half], sem)
        else:
            copy = pltpu.make_async_copy(w2h.at[0, pl.ds(at, W), :], w2.at[half], sem)
        copy.start()
        loads[which, half] = copy

    smalls = [
        pltpu.make_async_copy(src, dst, w_sem.at[4 + i])
        for i, (src, dst) in enumerate(((b_in_h, b_in), (b_out_h, b_out), (signs_h, signs_ref)))
    ]

    def need_smalls():
        while smalls:
            smalls.pop().wait()

    def need(which, half):
        copy = loads.pop((which, half), None)
        if copy is not None:
            copy.wait()

    def rows(index, size, part=None):
        start, count = (0, size) if part is None else part
        return pl.ds(pl.multiple_of(index * size + start, 16), count)

    def add_into(buf, first, others, count):
        @pl.loop(0, count // 16)
        def _(i):
            here = pl.ds(pl.multiple_of(first + i * 16, 16), 16)
            total = buf[here, :].astype(F32)
            for other, start in others:
                there = pl.ds(pl.multiple_of(start + i * 16, 16), 16)
                total = total + other[there, :].astype(F32)
            buf[here, :] = total.astype(BF)

    class Pair:
        def __init__(self, n):
            self.n = n
            self.first, self.t, self.tiles, self.out_tiles, self.straight, self.out_straight = PAIRS[n]
            self.wide = W // self.tiles
            for name in pair_scratch(n):
                setattr(self, name[: name.rindex("_")], named[name])

        def ways(self, odd, straight):
            t = self.t
            if straight:
                return None, (0, t), None, (0, t)
            if t >= 32:
                h = t // 2
                return (0, h), (h, t - h), (h, t - h), (0, h)
            return (None, (0, t), (0, t), None) if odd else ((0, t), None, None, (0, t))

    class Into:
        def __init__(self, pair, kind):
            self.q, self.kind = pair, kind
            self.forward = kind == FORWARD
            self.source = (tok if self.forward else cot).at[0]
            self.x = pair.x.at[kind]
            self.tag = f"i{pair.n}{kind}"
            self.up, self.up_rest, self.down, self.down_rest = pair.ways(not self.forward, pair.straight)

        def go(self, name, src, dst, target):
            go(self.tag + name, src, dst, target)

        def got(self, *names):
            got(*(self.tag + name for name in names))

        def part(self, p):
            return self.source.at[pl.ds(self.q.first + p[0], p[1])]

        def give(self, name, p, target):
            if p is not None:
                self.go(name, self.part(p), self.x.at[rows(row_id(0, 0), self.q.t, p)], target)

        def ag1(self, _):
            t = self.q.t
            self.give("x0", (0, t), "x")
            if self.q.straight:
                self.give("z2", (0, t), "z2")
            self.give("zpk", self.up, "z+")
            self.give("zmk", self.down, "z-")
            i = indices.setdefault(self.tag + "own", len(indices))
            self.own = pltpu.make_async_copy(
                self.part((0, t)), self.x.at[rows(row_id(0, 0), t)], send.at[i]
            )
            self.own.start()

        def ag1b(self, _):
            self.give("zpo", self.up_rest, "z+")
            self.give("zmo", self.down_rest, "z-")

        def pass_on(self, name, at, target):
            self.go(name, self.x.at[at], self.x.at[at], target)

        def ag2a(self, _):
            t = self.q.t
            if self.up is not None:
                self.got("zpk")
                self.pass_on("fp", rows(row_id(-1, 0), t, self.up), "z+")
            if self.down is not None:
                self.got("zmk")
                self.pass_on("fm", rows(row_id(1, 0), t, self.down), "z-")

        def ag2b(self, _):
            self.got("x0")
            peer = rows(row_id(0, 1), self.q.t)
            self.pass_on("zxp", peer, "z+")
            self.pass_on("zxm", peer, "z-")

        def ag3(self, _):
            self.got("fp", "fm", "z2")
            self.pass_on("x3", rows(row_id(2, 0), self.q.t), "x")

        def ag4(self, _):
            self.own.wait()
            self.got("zpo", "zmo", "zxp", "zxm", "x3")

        def into_hidden(self, half, tile, done):
            wide = self.q.wide
            for at in range(tile * wide, (tile + 1) * wide, TN):
                cols = pl.ds(at, TN)
                if self.forward:
                    value = jnp.dot(self.x[...], w1[half, :, cols], preferred_element_type=F32)
                else:
                    value = lax.dot_general(
                        self.x[...],
                        w2[half, cols, :],
                        (((1,), (1,)), ((), ())),
                        preferred_element_type=F32,
                    )
                done(pl.ds(at - tile * wide, TN), value)

        def a1(self, tile):
            need(1 if self.forward else 2, 1)
            ss, sr = self.q.ss.at[self.kind, tile], self.q.sr.at[self.kind, tile]

            def done(cols, value):
                ss[:, cols] = value.astype(BF)

            self.into_hidden(1, tile, done)
            self.go(f"ks{tile}", ss, sr, "k")

        def a2(self, tile):
            need(1 if self.forward else 2, 0)
            t, size = self.q.t, 2 * self.q.t
            c, sr, ra = (buf.at[self.kind, tile] for buf in (self.q.c, self.q.sr, self.q.ra))

            def done(cols, value):
                self.got(f"ks{tile}")
                c[:, cols] = (value + sr[:, cols].astype(F32)).astype(BF)

            self.into_hidden(0, tile, done)
            self.go(f"rap{tile}", c.at[rows(yo, size, (0, t))], ra.at[0], "y+")
            self.go(f"ram{tile}", c.at[rows(yo, size, (t, t))], ra.at[1], "y-")

        def rs1(self, tile):
            t, size = self.q.t, 2 * self.q.t
            c, rb = self.q.c.at[self.kind, tile], self.q.rb.at[self.kind, tile]
            self.go(f"rbpe{tile}", c.at[rows(yp, size, (t, t))], rb.at[0, pl.ds(t, t)], "y+")
            self.go(f"rbme{tile}", c.at[rows(ym, size, (0, t))], rb.at[1, pl.ds(0, t)], "y-")

        def rs2(self, tile):
            t, size = self.q.t, 2 * self.q.t
            c = self.q.c.at[self.kind, tile]
            ra, rb = self.q.ra.at[self.kind, tile], self.q.rb.at[self.kind, tile]
            self.got(f"rap{tile}")
            add_into(c, yp * size, [(ra.at[0], 0)], t)
            self.go(f"rbp{tile}", c.at[rows(yp, size, (0, t))], rb.at[0, pl.ds(0, t)], "y+")
            self.got(f"ram{tile}")
            add_into(c, ym * size + t, [(ra.at[1], 0)], t)
            self.go(f"rbm{tile}", c.at[rows(ym, size, (t, t))], rb.at[1, pl.ds(t, t)], "y-")

        def rs3(self, tile):
            size, wide = 2 * self.q.t, self.q.wide
            c, rb = self.q.c.at[self.kind, tile], self.q.rb.at[self.kind, tile]
            act, slope = self.q.act.at[self.kind, 0, tile], self.q.slope.at[tile]
            need_smalls()
            self.got(*(f"{name}{tile}" for name in ("rbpe", "rbme", "rbp", "rbm")))

            @pl.loop(0, size // 16)
            def _(i):
                here = pl.ds(pl.multiple_of(y * size + i * 16, 16), 16)
                piece = pl.ds(pl.multiple_of(i * 16, 16), 16)
                total = (
                    c[here, :].astype(F32) + rb[0, piece, :].astype(F32) + rb[1, piece, :].astype(F32)
                )
                if self.forward:
                    bias = b_in[:, pl.ds(pl.multiple_of(k * W + tile * wide, wide), wide)]
                    values, slopes = gelu_parts(total + bias)
                    slope[piece, :] = slopes
                else:
                    values = total * slope[piece, :]
                act[here, :] = values.astype(BF)

    class Out:
        def __init__(self, pair, slot):
            self.q, self.slot = pair, slot
            self.kind = s if slot == GOES else 1 - s
            self.act = pair.act.at[self.kind]
            self.number = pair.out_tiles[slot]
            self.wide = W // self.number
            self.p, self.rx, self.rza, self.rzb, self.rh = (
                getattr(pair, f"{name}{slot}") for name in ("p", "rx", "rza", "rzb", "rh")
            )
            self.tag = f"o{pair.n}{slot}"
            self.up, self.up_rest, self.down, self.down_rest = pair.ways(slot, pair.out_straight[slot])

        def go(self, name, src, dst, target):
            go(self.tag + name, src, dst, target)

        def got(self, *names):
            got(*(self.tag + name for name in names))

        def yg1(self, tile):
            t, size = self.q.t, 2 * self.q.t
            h0, h1 = rows(y, size, (0, t)), rows(y, size, (t, t))
            self.pass_on(f"gp0{tile}", tile, h0, "y+")
            self.pass_on(f"gm1{tile}", tile, h1, "y-")

        def yg1b(self, tile):
            t, size = self.q.t, 2 * self.q.t
            h0, h1 = rows(y, size, (0, t)), rows(y, size, (t, t))
            self.pass_on(f"gp1{tile}", tile, h1, "y+")
            self.pass_on(f"gm0{tile}", tile, h0, "y-")
            self.across(f"k0{tile}", tile, rows(y, size))

        def pass_on(self, name, tile, at, target):
            mine = self.act.at[0, tile, at]
            self.go(name, mine, mine, target)

        def across(self, name, tile, at):
            self.go(name, self.act.at[0, tile, at], self.act.at[1, tile, at], "k")

        def yg2(self, tile):
            t, size = self.q.t, 2 * self.q.t
            self.got(f"gp0{tile}")
            self.pass_on(f"hp{tile}", tile, rows(ym, size, (0, t)), "y+")
            self.got(f"gm1{tile}")
            self.pass_on(f"hm{tile}", tile, rows(yp, size, (t, t)), "y-")

        def yg3(self, tile):
            size = 2 * self.q.t
            self.got(f"gp1{tile}")
            self.across(f"k1{tile}", tile, rows(ym, size))
            self.got(f"gm0{tile}")
            self.across(f"k2{tile}", tile, rows(yp, size))

        def yg4(self, tile):
            t, size = self.q.t, 2 * self.q.t
            self.got(f"hp{tile}")
            self.across(f"k3{tile}", tile, rows(yo, size, (0, t)))
            self.got(f"hm{tile}")
            self.across(f"k4{tile}", tile, rows(yo, size, (t, t)))

        def product(self, kind, half, at):
            cols, wide = pl.ds(at, TN), self.q.wide
            total = None
            for tile in range(self.q.tiles):
                hidden = pl.ds(tile * wide, wide)
                if kind == FORWARD:
                    value = jnp.dot(
                        self.act[half, tile], w2[half, hidden, cols], preferred_element_type=F32
                    )
                else:
                    value = lax.dot_general(
                        self.act[half, tile],
                        w1[half, cols, hidden],
                        (((1,), (1,)), ((), ())),
                        preferred_element_type=F32,
                    )
                total = value if total is None else total + value
            return total

        def b(self, out):
            for which in (1, 2):
                for half in (0, 1):
                    need(which, half)
            settle(30)
            waits = [copies.pop(f"{self.tag}k{i}{tile}") for tile in range(self.q.tiles) for i in range(5)] if out == 0 else []
            p, t = self.p.at[out], self.q.t

            def tile_of(kind):
                for at in range(out * self.wide, (out + 1) * self.wide, TN):
                    total = self.product(kind, 0, at)
                    if at == 0:
                        for copy in waits:
                            copy.wait_recv()
                    total = total + self.product(kind, 1, at)
                    p[:, pl.ds(at - out * self.wide, TN)] = total.astype(BF)

            pl.when(self.kind == FORWARD)(functools.partial(tile_of, FORWARD))
            pl.when(self.kind == BACKWARD)(functools.partial(tile_of, BACKWARD))
            self.go(f"x1{out}", p.at[rows(row_id(2, 1), t)], self.rx.at[out, 0], "x")
            self.go(f"zap{out}", p.at[rows(row_id(1, 1), t)], self.rza.at[out, 0], "z+")
            self.go(f"zam{out}", p.at[rows(row_id(-1, 1), t)], self.rza.at[out, 1], "z-")

        def rr1(self, out):
            self.give_sum(f"zbpe{out}", out, row_id(1, 0), self.up_rest, 0, "z+")
            self.give_sum(f"zbme{out}", out, row_id(-1, 0), self.down_rest, 1, "z-")

        def give_sum(self, name, out, row, part, side, target):
            if part is not None:
                self.go(
                    name,
                    self.p.at[out, rows(row, self.q.t, part)],
                    self.rzb.at[out, side, pl.ds(*part)],
                    target,
                )

        def rr2a(self, out):
            t, p, far = self.q.t, self.p.at[out], row_id(2, 0)
            self.got(f"x1{out}")
            add_into(p, far * t, [(self.rx.at[out, 0], 0)], t)
            for name, part, target in (("zhp", self.up, "z+"), ("zhm", self.down, "z-")):
                if part is not None:
                    self.go(f"{name}{out}", p.at[rows(far, t, part)], self.rh.at[out, pl.ds(*part)], target)
            if self.q.out_straight[self.slot]:
                self.go(f"z2{out}", p.at[rows(far, t)], self.rh.at[out], "z2")

        def rr2b(self, out):
            t, p, peer = self.q.t, self.p.at[out], row_id(0, 1)
            self.got(f"zap{out}", f"zam{out}")
            add_into(p, peer * t, [(self.rza.at[out, 0], 0), (self.rza.at[out, 1], 0)], t)
            self.go(f"x2{out}", p.at[rows(peer, t)], self.rx.at[out, 1], "x")

        def rr3(self, out):
            t, p, rh = self.q.t, self.p.at[out], self.rh.at[out]
            settle(16)
            if self.up is not None:
                self.got(f"zhp{out}")
                add_into(p, row_id(1, 0) * t + self.up[0], [(rh, self.up[0])], self.up[1])
                self.give_sum(f"zbp{out}", out, row_id(1, 0), self.up, 0, "z+")
            if self.down is not None:
                self.got(f"zhm{out}")
                add_into(p, row_id(-1, 0) * t + self.down[0], [(rh, self.down[0])], self.down[1])
                self.give_sum(f"zbm{out}", out, row_id(-1, 0), self.down, 1, "z-")

        def rr4(self, out):
            t, wide = self.q.t, self.wide
            self.got(*(f"{name}{out}" for name in ("zbpe", "zbme", "zbp", "zbm", "x2", "z2")))
            mine = rows(row_id(0, 0), t)
            cols = pl.ds(out * wide, wide)
            total = (
                self.p[out, mine, :].astype(F32)
                + self.rzb[out, 0].astype(F32)
                + self.rzb[out, 1].astype(F32)
                + self.rx[out, 1].astype(F32)
                + self.q.x[self.kind, mine, cols].astype(F32)
            )
            if self.q.out_straight[self.slot]:
                total = total + self.rh[out].astype(F32)
            total = total + jnp.where(self.kind == FORWARD, b_out[:, cols], 0.0)
            if self.slot == STAYS:
                stayed[pl.ds(self.q.first, t), cols] = total.astype(BF)
                return
            stacked = blocks_down(total)
            high = stacked.astype(BF)
            rest = stacked - high.astype(F32)
            mid = rest.astype(BF)
            low = (rest - mid.astype(F32)).astype(BF)
            signs = signs_ref[...]
            turned = turn(high, signs) + (turn(mid, signs) + turn(low, signs))
            turned = turned * (1.0 / math.sqrt(HB))
            self.q.out[:, cols] = blocks_back(turned, t).astype(BF)
            self.go(f"sec{out}", self.q.out.at[:, cols], self.q.inn.at[:, cols], "s")

        def fin(self, _):
            self.got(*(f"sec{out}" for out in range(self.number)))
            came[pl.ds(self.q.first, self.q.t), :] = self.q.inn[...]

    barrier = pltpu.get_barrier_semaphore()
    for target in to.values():
        pl.semaphore_signal(barrier, inc=1, device_id=target, device_id_type=pl.DeviceIdType.MESH)
    for which, half in ((1, 1), (1, 0), (2, 1), (2, 0)):
        load_weights(which, half)
    for copy in smalls:
        copy.start()

    pl.semaphore_wait(barrier, len(to))

    jobs = []
    for n in range(len(PAIRS)):
        pair = Pair(n)
        jobs.append((Into(pair, FORWARD), Into(pair, BACKWARD), Out(pair, GOES), Out(pair, STAYS)))
    for step in ORDER:
        phase, job = PHASES[step // 32], jobs[step // 8 % 4][step // 2 % 4]
        getattr(job, phase)(step % 2)
    settle(0)


def finish_kernel(came, stayed, signs, handed, leaving):
    turned = turn(blocks_down(came[...]), signs[...]) * (1.0 / math.sqrt(HB))
    handed[0] = blocks_back(turned, came.shape[0])
    leaving[0] = stayed[...]


def on_device(tokens, cotangent, w_in, b_in, w_out, b_out):
    scratch = dict(
        w1=pltpu.VMEM((2, W, W), BF),
        w2=pltpu.VMEM((2, W, W), BF),
        w_sem=pltpu.SemaphoreType.DMA((7,)),
        b_in=pltpu.VMEM(b_in.shape, F32),
        b_out=pltpu.VMEM(b_out.shape, F32),
        signs=pltpu.VMEM((HB, HB), BF),
        send=pltpu.SemaphoreType.DMA((SEMAPHORES,)),
        recv=pltpu.SemaphoreType.DMA((SEMAPHORES,)),
    )
    for n in range(len(PAIRS)):
        scratch.update(pair_scratch(n))
    signs = jnp.asarray(hadamard_signs(HB), BF)
    vmem, anywhere = pl.BlockSpec(memory_space=pltpu.VMEM), pl.BlockSpec(memory_space=pl.ANY)
    tile = jax.ShapeDtypeStruct(tokens.shape[1:], BF)
    came, stayed = pl.pallas_call(
        functools.partial(kernel, tuple(scratch)),
        out_shape=(tile, tile),
        in_specs=[anywhere] * 7,
        out_specs=(vmem, vmem),
        scratch_shapes=list(scratch.values()),
        cost_estimate=pl.CostEstimate(flops=19_500_000_000, bytes_accessed=20_000_000, transcendentals=200_000),
        compiler_params=pltpu.CompilerParams(
            collective_id=0, has_side_effects=True, vmem_limit_bytes=56 << 20
        ),
        name="feed_forward",
    )(tokens, cotangent, w_in, b_in, w_out, b_out, signs)
    return pl.pallas_call(
        finish_kernel,
        out_shape=(
            jax.ShapeDtypeStruct(tokens.shape, F32),
            jax.ShapeDtypeStruct(tokens.shape, BF),
        ),
        in_specs=[vmem, vmem, vmem],
        out_specs=(vmem, vmem),
        name="hand_over",
    )(came, stayed, signs)


def solution(mesh):
    in_specs = (
        P("section", "row", "col"),
        P("section", "row", "col"),
        P("section", "col", "row"),
        P("section", "row"),
        P("section", "row", "col"),
        P("section", "col"),
    )
    out_specs = (P("section", "row", "col"), P("section", "row", "col"))
    return jax.shard_map(
        on_device, mesh=mesh, in_specs=in_specs, out_specs=out_specs, check_vma=False
    )
```
